128 devices in a mesh: aux: 16 (over y, x), obat: 8 (over z, core).
Axes of the slice: x: 4, y: 4, z: 4, core: 2. Of those that a mesh axis runs over, the one named last changes fastest.
Arguments:
- half_factors: bfloat16 [2048, 128, 768], P('aux', 'obat'), may hold values from -2 to 2
- block_mask: int32 [128, 12], P('obat'), may hold values 0 or 1
- virt_coef: bfloat16 [768, 512], replicated, may hold values from -0.21875 to 0.21875
- occ_energy: float32 [128], replicated, may hold values from -2 to -0.4
- virt_energy: float32 [512], replicated, may hold values from 0.3 to 3
- pair_list: int32 [128, 6], replicated, may hold values from 0 to 127, as said below
- pair_count: int32 [128], replicated, may hold values from 1 to 6
Outputs:
- gamma_ao: float32 [2048, 128, 768], P('aux', 'obat')
The draws below stay inside these ranges and needn't reach their ends.
Inputs may be any that keep to these rules, and one draw needn't show every extreme that they name: `pair_list`: row i holds 6 different orbitals j, each with j % 16 // 1 equal to i % 16; only its first pair_count[i] entries are used.
All inputs are finite; a program needn't handle non-finite values. No bound on the sum of `block_mask` on one device may be relied on, other than what follows from the above.
Results may differ from the reference program's by a relative error of at most 0.0037.
Values may be sent and summed in bfloat16 or wider, within the bound.
A program may use at most 128 MiB of HBM per device.

```python
import jax
import jax.numpy as jnp
from jax import lax

NAUX = 2048
NAO = 768
NVIR = 512
OB = 16
AOBLK = 64
JCAP = 6
NOCC = 128
OL = 1
PEERS = 8
NBLK = 12


def draw_pair_list(key, part):
    orbitals = jnp.arange(NOCC, dtype=jnp.int32)
    group_of = orbitals % OB // OL
    row_keys = jax.random.split(key, NOCC)
    picks = jax.vmap(lambda one_key: jax.random.permutation(one_key, PEERS)[:JCAP])(row_keys).astype(jnp.int32)
    batch_of = picks // OL
    within = picks % OL
    return (batch_of * OB + group_of[:, None] * OL + within).astype(jnp.int32)


def draw_pair_count(key, part):
    counts = jax.random.randint(key, (NOCC,), 1, JCAP + 1)
    chosen = jax.random.randint(jax.random.fold_in(key, 7), (), 0, NOCC)
    return jnp.where(jnp.arange(NOCC) == chosen, JCAP, counts).astype(jnp.int32)


def plant(entries, key, low, high):
    extent = entries.shape
    place = [jax.random.randint(jax.random.fold_in(key, axis), (), 0, extent[axis]) for axis in range(len(extent))]
    entries = entries.at[tuple(place)].set(low)
    longest = extent.index(max(extent))
    place[longest] = (place[longest] + 1) % extent[longest]
    return entries.at[tuple(place)].set(high)


def levels(key, shape, cuts, least, top_value):
    factor_of = 1.0
    for position, shards_of in cuts:
        draws = jax.random.uniform(jax.random.fold_in(jax.random.fold_in(key, 6), position), (shards_of,), jnp.float32, least / len(cuts), top_value / len(cuts))
        factor_of = factor_of * jnp.repeat(jnp.exp(draws), shape[position] // shards_of).reshape((-1,) + (1,) * (len(shape) - 1 - position))
    return factor_of


def bell_draw(stream_key, dims, scale, most, cuts=(), kind=jnp.bfloat16):
    entries = jax.random.normal(stream_key, dims, jnp.float32) * scale
    if len(cuts) > 0:
        entries = levels(stream_key, dims, cuts, -0.22, 0.18) * entries
    return jnp.clip(entries, min=-most, max=most).astype(kind)


def setup_inputs(seed: int = 0) -> dict:
    arg_keys = jax.random.split(jax.random.key(seed), 8)
    return {
        "half_factors": bell_draw(arg_keys[0], (NAUX, NOCC, NAO), 0.15, 2.0, ((0, 16), (1, 8))),
        "block_mask": plant((jax.random.randint(arg_keys[1], (NOCC, NBLK), 0, 4) < 3).astype(jnp.int32), jax.random.fold_in(arg_keys[1], 1), 0, 1),
        "virt_coef": bell_draw(arg_keys[2], (NAO, NVIR), NAO ** -0.5, 0.21875),
        "occ_energy": jnp.clip(jax.random.uniform(arg_keys[3], (NOCC,), jnp.float32, -2.0, -0.4), -2.0, -0.4),
        "virt_energy": jnp.clip(jax.random.uniform(arg_keys[4], (NVIR,), jnp.float32, 0.3, 3.0), 0.3, 3.0),
        "pair_list": draw_pair_list(jax.random.fold_in(arg_keys[7], 71), 0),
        "pair_count": draw_pair_count(jax.random.fold_in(arg_keys[7], 71), 0),
    }


def reference(half_factors, block_mask, virt_coef, occ_energy, virt_energy, pair_list, pair_count):
    expand = jnp.repeat(block_mask, AOBLK, axis=1).astype(jnp.bfloat16)

    def transform(items):
        rows, mask_row = items
        masked = rows * mask_row[None, :]
        return jnp.dot(masked, virt_coef, preferred_element_type=jnp.float32).astype(jnp.bfloat16)

    factors = lax.map(transform, (jnp.moveaxis(half_factors, 1, 0), expand))

    def one_orbital(items):
        own_panel, own_energy, listed, counted = items

        def add_pair(index, total):
            partner_id = listed[index]
            partner = factors[partner_id]
            integrals = lax.dot_general(own_panel, partner, (((0,), (0,)), ((), ())), preferred_element_type=jnp.float32)
            denom = own_energy + occ_energy[partner_id] - virt_energy[:, None] - virt_energy[None, :]
            amplitude = integrals / denom
            mixed = (2.0 * amplitude - amplitude.T).astype(jnp.bfloat16)
            return total + lax.dot_general(partner, mixed, (((1,), (1,)), ((), ())), preferred_element_type=jnp.float32)

        start = jnp.zeros((NAUX, NVIR), jnp.float32)
        return lax.fori_loop(jnp.int32(0), counted.astype(jnp.int32), add_pair, start)

    gamma = lax.map(one_orbital, (factors, occ_energy, pair_list, pair_count))

    def back_transform(panel):
        return jnp.dot(panel.astype(jnp.bfloat16), virt_coef.T, preferred_element_type=jnp.float32)

    gamma_ao = lax.map(back_transform, gamma)
    return jnp.moveaxis(gamma_ao, 0, 1)
```

```python
import jax
import jax.numpy as jnp
from jax import lax
from jax.sharding import PartitionSpec as P

AOBLK = 64


def on_device(half_factors, block_mask, virt_coef, occ_energy, virt_energy, pair_list, pair_count):
    batch_rows = half_factors.shape[1]
    expand = jnp.repeat(block_mask, AOBLK, axis=1).astype(jnp.bfloat16)
    masked = half_factors * expand[None, :, :]
    local = jnp.einsum(
        "pim,ma->ipa", masked, virt_coef, preferred_element_type=jnp.float32
    ).astype(jnp.bfloat16)
    own_panel = lax.all_to_all(local, "aux", split_axis=0, concat_axis=1, tiled=True)[0]
    panels = lax.all_gather(own_panel, "obat", axis=0, tiled=False)
    orbital = lax.axis_index("obat") * batch_rows + lax.axis_index("aux")
    own_energy = lax.dynamic_index_in_dim(occ_energy, orbital, 0, keepdims=False)
    listed = lax.dynamic_index_in_dim(pair_list, orbital, 0, keepdims=False)
    counted = lax.dynamic_index_in_dim(pair_count, orbital, 0, keepdims=False)

    def add_pair(index, total):
        partner_id = lax.dynamic_index_in_dim(listed, index, 0, keepdims=False)
        partner = lax.dynamic_index_in_dim(panels, partner_id // batch_rows, 0, keepdims=False)
        integrals = lax.dot_general(
            own_panel, partner, (((0,), (0,)), ((), ())), preferred_element_type=jnp.float32
        )
        partner_energy = lax.dynamic_index_in_dim(occ_energy, partner_id, 0, keepdims=False)
        denom = own_energy + partner_energy - virt_energy[:, None] - virt_energy[None, :]
        mixed = ((2.0 * integrals - integrals.T) / denom).astype(jnp.bfloat16)
        return total + lax.dot_general(
            partner, mixed, (((1,), (1,)), ((), ())), preferred_element_type=jnp.float32
        )

    start = jnp.zeros(own_panel.shape, jnp.float32)
    gamma = lax.fori_loop(jnp.int32(0), counted, add_pair, start)
    gamma_low = gamma.astype(jnp.bfloat16)[None]
    back = lax.all_to_all(gamma_low, "aux", split_axis=1, concat_axis=0, tiled=True)
    return jnp.einsum("ipa,ma->pim", back, virt_coef, preferred_element_type=jnp.float32)


def solution(mesh):
    in_specs = (P("aux", "obat", None), P("obat", None), P(), P(), P(), P(), P())
    out_specs = P("aux", "obat", None)
    return jax.shard_map(
        on_device, mesh=mesh, in_specs=in_specs, out_specs=out_specs, check_vma=False
    )
```

```python
import functools

import jax
import jax.numpy as jnp
from jax import lax
from jax.experimental import pallas as pl
from jax.experimental.pallas import tpu as pltpu
from jax.sharding import PartitionSpec as P

AOBLK = 64
SIDE = 4
LAG = (1, 3, 5, 6)
MESH = pl.DeviceIdType.MESH


def dot(a, b):
    return lax.dot_general(a, b, (((1,), (0,)), ((), ())), preferred_element_type=jnp.float32)


def pair_kernel(
    sums, weight, virt_row, virt_col, local, out,
    panels, total, recip, mixed, gamma,
    a_send, a_recv, u_send, u_recv, d_send, d_recv, f_send, f_recv, s_send, s_recv, r_send, r_recv,
):
    aux = lax.axis_index("aux")
    obat = lax.axis_index("obat")
    y, x = aux // SIDE, aux % SIDE
    z, core = obat // 2, obat % 2
    rounds, slab = local.shape[0], local.shape[1]
    nvir = local.shape[2]
    slots = panels.shape[0]
    above = (aux, (z + 1) % SIDE * 2 + core)
    below = (aux, (z + SIDE - 1) % SIDE * 2 + core)
    sibling = (aux, z * 2 + 1 - core)
    chunks = rounds // 2
    wide = 2 * slab

    def target(r):
        return (y + r // SIDE) % SIDE * SIDE + (x + r % SIDE) % SIDE

    def source(r):
        return (y + SIDE - r // SIDE) % SIDE * SIDE + (x + SIDE - r % SIDE) % SIDE

    def rows(r):
        return pl.ds(pl.multiple_of(r * slab, slab), slab)

    def push(src, dst, send, recv, device):
        return pltpu.make_async_remote_copy(
            src_ref=src, dst_ref=dst, send_sem=send, recv_sem=recv,
            device_id=device, device_id_type=MESH,
        )

    def scatter(r):
        return push(local.at[target(r)], panels.at[0, rows(r)], a_send.at[r], a_recv.at[r], (target(r), obat))

    def upward(r):
        return push(panels.at[0, rows(r)], panels.at[2, rows(r)], u_send.at[r], u_recv.at[r], above)

    def downward(r):
        return push(panels.at[0, rows(r)], panels.at[4, rows(r)], d_send.at[r], d_recv.at[r], below)

    def further_up(r):
        return push(panels.at[2, rows(r)], panels.at[6, rows(r)], f_send.at[r], f_recv.at[r], above)

    def further_down(r):
        return push(panels.at[4, rows(r)], panels.at[6, rows(r)], f_send.at[r], f_recv.at[r], below)

    def across(k, r):
        return push(
            panels.at[2 * k, rows(r)], panels.at[2 * k + 1, rows(r)],
            s_send.at[k, r], s_recv.at[k, r], sibling,
        )

    def back(r):
        return push(gamma.at[rows(r)], out.at[aux], r_send.at[r], r_recv.at[r], (source(r), obat))

    barrier = pltpu.get_barrier_semaphore()

    def greet(r, carry):
        pl.semaphore_signal(barrier, inc=1, device_id=(target(r), obat), device_id_type=MESH)
        return carry

    lax.fori_loop(1, rounds, greet, 0)
    for device in (above, below, sibling):
        pl.semaphore_signal(barrier, inc=1, device_id=device, device_id_type=MESH)
    pl.semaphore_wait(barrier, rounds + 2)

    def send_out(r, carry):
        scatter(r).start()
        return carry

    lax.fori_loop(1, rounds, send_out, 0)
    panels[0, pl.ds(0, slab), :] = local[aux]

    def prepare(s, carry):
        total[s] = jnp.zeros((nvir, nvir), jnp.float32)
        denom = (sums[s] - virt_col[...]) - virt_row[...]
        recip[s] = weight[s] / denom
        return carry

    def pair_up(k, c):
        part = pl.ds(pl.multiple_of(c * wide, wide), wide)
        own = panels[0, part, :]
        flipped = (-own).T
        for s in (2 * k, 2 * k + 1):
            other = panels[s, part, :]
            total[s] += dot((2 * other).T, own) + dot(flipped, other)

    def stage(c, carry):
        @pl.when(c < chunks)
        def _():
            for h in range(2):
                r = 2 * c + h
                if h == 0:
                    @pl.when(r > 0)
                    def _():
                        scatter(r).wait_recv()
                else:
                    scatter(r).wait_recv()
                upward(r).start()
                downward(r).start()
                across(0, r).start()

        @pl.when((c >= LAG[0]) & (c < chunks + LAG[0]))
        def _():
            for h in range(2):
                r = 2 * (c - LAG[0]) + h
                upward(r).wait_recv()
                downward(r).wait_recv()
                if h == 0:
                    further_up(r).start()
                else:
                    further_down(r).start()
                across(1, r).start()
                across(2, r).start()

        @pl.when(c == 0)
        def _():
            lax.fori_loop(0, slots, prepare, 0)

        @pl.when((c >= LAG[0]) & (c < chunks + LAG[0]))
        def _():
            b = c - LAG[0]
            for h in range(2):
                across(0, 2 * b + h).wait_recv()
            pair_up(0, b)

        @pl.when((c >= LAG[1]) & (c < chunks + LAG[1]))
        def _():
            b = c - LAG[1]
            for h in range(2):
                further_up(2 * b + h).wait_recv()
                across(3, 2 * b + h).start()
            for k in (1, 2):
                for h in range(2):
                    across(k, 2 * b + h).wait_recv()
                pair_up(k, b)

        @pl.when((c >= LAG[2]) & (c < chunks + LAG[2]))
        def _():
            b = c - LAG[2]
            for h in range(2):
                across(3, 2 * b + h).wait_recv()
            pair_up(3, b)

        return carry

    lax.fori_loop(0, chunks + LAG[2], stage, 0)

    def finish(s, carry):
        mixed[s] = (total[s] * recip[s]).astype(jnp.bfloat16)
        return carry

    lax.fori_loop(0, slots, finish, 0)

    def collect(q, carry):
        quarter = rounds // SIDE - 1 - q
        part = pl.ds(pl.multiple_of(quarter * SIDE * slab, SIDE * slab), SIDE * slab)
        for n in range(2):
            cols = pl.ds(n * (nvir // 2), nvir // 2)
            acc = dot(panels[0, part, :], mixed[0, :, cols])
            for s in range(1, slots):
                acc += dot(panels[s, part, :], mixed[s, :, cols])
            gamma[part, cols] = acc.astype(jnp.bfloat16)
        for h in range(SIDE):
            r = quarter * SIDE + h
            if h == 0:
                @pl.when(r > 0)
                def _():
                    back(r).start()
            else:
                back(r).start()
        return carry

    lax.fori_loop(0, rounds // SIDE, collect, 0)
    own_copy = pltpu.make_async_copy(gamma.at[pl.ds(0, slab)], out.at[aux], r_send.at[0])
    own_copy.start()

    def settle(r, carry):
        upward(r).wait_send()
        downward(r).wait_send()
        further_up(r).wait_send()
        for k in range(slots // 2):
            across(k, r).wait_send()
        return carry

    lax.fori_loop(0, rounds, settle, 0)

    def close(r, carry):
        scatter(r).wait_send()
        back(r).wait()
        return carry

    own_copy.wait()
    lax.fori_loop(1, rounds, close, 0)


def on_device(half_factors, block_mask, virt_coef, occ_energy, virt_energy, pair_list, pair_count):
    slab, batch_rows, _ = half_factors.shape
    nvir = virt_coef.shape[1]
    expand = jnp.repeat(block_mask, AOBLK, axis=1).astype(jnp.bfloat16)
    masked = half_factors * expand[None, :, :]
    local = jnp.einsum(
        "pim,ma->ipa", masked, virt_coef, preferred_element_type=jnp.float32
    ).astype(jnp.bfloat16)

    aux, obat = lax.axis_index("aux"), lax.axis_index("obat")
    z, core = obat // 2, obat % 2
    orbital = obat * batch_rows + aux
    step = jnp.array([0, 0, -1, -1, 1, 1, 2, 2], jnp.int32)
    other = jnp.array([0, 1] * 4, jnp.int32)
    batch = (z + step + SIDE) % SIDE * 2 + (core + other) % 2
    member = batch * batch_rows + aux
    sums = occ_energy[orbital] + occ_energy[member]
    used = jnp.arange(pair_list.shape[1]) < pair_count[orbital]
    weight = jnp.any((pair_list[orbital][None, :] == member[:, None]) & used[None, :], axis=1)
    weight = weight.astype(jnp.float32)

    rounds, slots = batch_rows, 8
    length = rounds * slab
    dma = pltpu.SemaphoreType.DMA
    smem = pl.BlockSpec(memory_space=pltpu.SMEM)
    vmem = pl.BlockSpec(memory_space=pltpu.VMEM)
    back = pl.pallas_call(
        pair_kernel,
        out_shape=jax.ShapeDtypeStruct((rounds, slab, nvir), jnp.bfloat16),
        in_specs=[smem, smem, vmem, vmem, vmem],
        out_specs=pl.BlockSpec(memory_space=pl.ANY),
        scratch_shapes=[
            pltpu.VMEM((slots, length, nvir), jnp.bfloat16),
            pltpu.VMEM((slots, nvir, nvir), jnp.float32),
            pltpu.VMEM((slots, nvir, nvir), jnp.float32),
            pltpu.VMEM((slots, nvir, nvir), jnp.bfloat16),
            pltpu.VMEM((length, nvir), jnp.bfloat16),
        ]
        + [dma((rounds,))] * 8
        + [dma((slots // 2, rounds))] * 2
        + [dma((rounds,))] * 2,
        compiler_params=pltpu.CompilerParams(
            collective_id=0, has_side_effects=True, vmem_limit_bytes=60 * 1024 * 1024
        ),
    )(sums, weight, virt_energy[None, :], virt_energy[:, None], local)
    return jnp.einsum("ipa,ma->pim", back, virt_coef, preferred_element_type=jnp.float32)


def solution(mesh):
    in_specs = (P("aux", "obat", None), P("obat", None), P(), P(), P(), P(), P())
    out_specs = P("aux", "obat", None)
    return jax.shard_map(
        on_device, mesh=mesh, in_specs=in_specs, out_specs=out_specs, check_vma=False
    )
```

```python
import jax
import jax.numpy as jnp
from jax import lax
from jax.experimental import pallas as pl
from jax.experimental.pallas import tpu as pltpu
from jax.sharding import PartitionSpec as P

AOBLK = 64
SIDE = 4
AHEAD = 3
LAG_NEAR, LAG_FAR = 1, 2
LOADS = 4
MESH = pl.DeviceIdType.MESH


def dot(a, b, contract=((1,), (0,))):
    return lax.dot_general(a, b, (contract, ((), ())), preferred_element_type=jnp.float32)


def pair_kernel(
    occ, listed, counted, mask, virt_row, virt, half, out,
    half_vm, wide_f, local, panels, total, recip, mixed, share, opposite, gamma, virt_col, sums, weight,
    l_sem, a_send, a_recv, m_send, m_recv, p_send, p_recv, s_send, s_recv, g_send, g_recv, r_send, r_recv,
):
    aux = lax.axis_index("aux")
    obat = lax.axis_index("obat")
    y, x = aux // SIDE, aux % SIDE
    z, core = obat // 2, obat % 2
    rounds, slab, nvir = local.shape
    slots = total.shape[0]
    lanes = nvir // 128
    chunks = rounds // 2
    wide = 2 * slab
    z_one = (z + SIDE - 1 + 2 * core) % SIDE
    z_two = (z + 1 + 2 * core) % SIDE
    one = (aux, z_one * 2 + core)
    two = (aux, z_two * 2 + core)
    sibling = (aux, z * 2 + 1 - core)

    def shift(r):
        return (r + r // SIDE) % SIDE, r % SIDE

    def target(r):
        dy, dx = shift(r)
        return (y + dy) % SIDE * SIDE + (x + dx) % SIDE

    def source(r):
        dy, dx = shift(r)
        return (y + SIDE - dy) % SIDE * SIDE + (x + SIDE - dx) % SIDE

    def rows(r):
        return pl.ds(pl.multiple_of(r * slab, slab), slab)

    def push(src, dst, send, recv, device):
        return pltpu.make_async_remote_copy(
            src_ref=src, dst_ref=dst, send_sem=send, recv_sem=recv,
            device_id=device, device_id_type=MESH,
        )

    def scatter(r):
        return push(local.at[r], panels.at[0, rows(r)], a_send.at[r], a_recv.at[r], (target(r), obat))

    def to_one(r):
        return push(panels.at[0, rows(r)], panels.at[4, rows(r)], m_send.at[r], m_recv.at[r], one)

    def to_two(r):
        return push(panels.at[0, rows(r)], panels.at[2, rows(r)], p_send.at[r], p_recv.at[r], two)

    def across(k, r):
        return push(
            panels.at[2 * k, rows(r)], panels.at[(1, 5, 3)[k], rows(r)],
            s_send.at[k, r], s_recv.at[k, r], sibling,
        )

    def give(r):
        return push(share.at[rows(r)], opposite.at[rows(r)], g_send.at[r], g_recv.at[r], one)

    def back(r):
        return push(gamma.at[rows(r)], out.at[aux], r_send.at[r], r_recv.at[r], (source(r), obat))

    piece = slab // LOADS

    def load(n):
        part = pl.ds(n * piece, piece)
        return pltpu.make_async_copy(half.at[part], half_vm.at[part], l_sem.at[n])

    for n in range(LOADS):
        load(n).start()

    barrier = pltpu.get_barrier_semaphore()

    def greet(r, carry):
        pl.semaphore_signal(barrier, inc=1, device_id=(target(r), obat), device_id_type=MESH)
        return carry

    lax.fori_loop(1, rounds, greet, 0)
    for device in (one, two, sibling):
        pl.semaphore_signal(barrier, inc=1, device_id=device, device_id_type=MESH)

    blocks = mask.shape[1]
    nao = virt.shape[0]
    spread = lax.broadcasted_iota(jnp.int32, (blocks, nao), 1) // AOBLK
    spread = (spread == lax.broadcasted_iota(jnp.int32, (blocks, nao), 0)).astype(jnp.bfloat16)
    keep = dot(mask[...].astype(jnp.bfloat16), spread).astype(jnp.bfloat16)
    for n in range(LOADS):
        load(n).wait()
        block = half_vm[pl.ds(n * piece, piece)] * keep[None]
        block = block.reshape(piece * rounds, nao)
        product = dot(block, virt[...])
        for w in range(lanes):
            wide_f[w, pl.ds(n * piece * rounds, piece * rounds), :] = product[:, w * 128 : (w + 1) * 128]

    def pick(r):
        parts = [wide_f[w, pl.ds(target(r), slab, stride=rounds), :] for w in range(lanes)]
        return jnp.concatenate(parts, axis=1).astype(jnp.bfloat16)

    panels[0, pl.ds(0, slab), :] = pick(0)
    pl.semaphore_wait(barrier, rounds + 2)

    def send_out(r, carry):
        local[r] = pick(r)
        scatter(r).start()
        return carry

    lax.fori_loop(1, 2 * AHEAD, send_out, 0)

    def orbital(level, side):
        return (level * 2 + side) * rounds + aux

    mine, foreign = orbital(z, core), orbital(z_one, core)
    couples = [(mine, orbital(level, side)) for level in (z, z_one, z_two) for side in (core, 1 - core)]
    couples += [(foreign, orbital(z_two, side)) for side in (core, 1 - core)]

    def prepare_scalars():
        for s, (i, j) in enumerate(couples):
            sums[s] = occ[i] + occ[j]
            hit = jnp.int32(0)
            for p in range(listed.shape[1]):
                hit += jnp.where((listed[i, p] == j) & (p < counted[i]), 1, 0)
            weight[s] = hit.astype(jnp.float32)

    def prepare(s, carry):
        total[s] = jnp.zeros((nvir, nvir), jnp.float32)
        for n in range(nvir // 128):
            cols = pl.ds(n * 128, 128)
            denom = (sums[s] - virt_col[...]) - virt_row[:, cols]
            recip[s, :, cols] = weight[s] / denom
        return carry

    def pair_up(c, held, fixed, others):
        part = pl.ds(pl.multiple_of(c * wide, wide), wide)
        own = panels[fixed, part, :]
        flipped = (-own).T
        for t, s in zip(held, others):
            other = panels[s, part, :]
            total[t] += dot((2 * other).T, own) + dot(flipped, other)

    def stage(c, carry):
        @pl.when(c < chunks)
        def _():
            for h in range(2):
                r = 2 * c + h
                if h == 0:
                    @pl.when(r > 0)
                    def _():
                        scatter(r).wait_recv()
                else:
                    scatter(r).wait_recv()
                to_one(r).start()
                to_two(r).start()
                across(0, r).start()

        @pl.when(c + AHEAD < chunks)
        def _():
            for h in range(2):
                send_out(2 * (c + AHEAD) + h, 0)

        @pl.when((c >= LAG_NEAR) & (c < chunks + LAG_NEAR))
        def _():
            for h in range(2):
                r = 2 * (c - LAG_NEAR) + h
                to_two(r).wait_recv()
                across(1, r).start()
                to_one(r).wait_recv()
                across(2, r).start()

        @pl.when(c == 0)
        def _():
            virt_col[...] = jnp.broadcast_to(virt_row[...], (128, nvir)).T
            prepare_scalars()
            lax.fori_loop(0, slots, prepare, 0)

        @pl.when((c >= LAG_NEAR) & (c < chunks + LAG_NEAR))
        def _():
            b = c - LAG_NEAR
            for h in range(2):
                across(0, 2 * b + h).wait_recv()
            pair_up(b, (0, 1, 2, 4), 0, (0, 1, 2, 4))
            pair_up(b, (6,), 2, (4,))

        @pl.when(c >= LAG_FAR)
        def _():
            b = c - LAG_FAR
            for h in range(2):
                across(1, 2 * b + h).wait_recv()
                across(2, 2 * b + h).wait_recv()
            pair_up(b, (3, 5), 0, (3, 5))
            pair_up(b, (7,), 2, (5,))

        return carry

    lax.fori_loop(0, chunks + LAG_FAR, stage, 0)

    def finish(t, carry):
        s = slots - 1 - t
        mixed[s] = (total[s] * recip[s]).astype(jnp.bfloat16)
        return carry

    lax.fori_loop(0, slots, finish, 0)

    halves = [pl.ds(n * (nvir // 2), nvir // 2) for n in range(2)]

    def hand_over(q, carry):
        length = SIDE * slab
        quarter = rounds // SIDE - 1 - q
        part = pl.ds(pl.multiple_of(quarter * length, length), length)
        for cols in halves:
            acc = dot(panels[4, part, :], mixed[6, :, cols]) + dot(panels[5, part, :], mixed[7, :, cols])
            share[part, cols] = acc.astype(jnp.bfloat16)
        for h in range(SIDE):
            give(quarter * SIDE + SIDE - 1 - h).start()
        return carry

    lax.fori_loop(0, rounds // SIDE, hand_over, 0)

    def collect(q, carry):
        c = chunks - 1 - q
        part = pl.ds(pl.multiple_of(c * wide, wide), wide)
        give(2 * c + 1).wait_recv()
        give(2 * c).wait_recv()
        for cols in halves:
            acc = opposite[part, cols].astype(jnp.float32)
            for s in range(6):
                acc += dot(panels[s, part, :], mixed[s, :, cols])
            gamma[part, cols] = acc.astype(jnp.bfloat16)
        back(2 * c + 1).start()

        @pl.when(c > 0)
        def _():
            back(2 * c).start()

        return carry

    lax.fori_loop(0, chunks, collect, 0)
    own_copy = pltpu.make_async_copy(gamma.at[pl.ds(0, slab)], out.at[aux], r_send.at[0])
    own_copy.start()

    def settle(r, carry):
        to_one(r).wait_send()
        to_two(r).wait_send()
        give(r).wait_send()
        for k in range(3):
            across(k, r).wait_send()
        return carry

    lax.fori_loop(0, rounds, settle, 0)

    def close(r, carry):
        scatter(r).wait_send()
        back(r).wait()
        return carry

    own_copy.wait()
    lax.fori_loop(1, rounds, close, 0)


def last_kernel(back, virt, out, mixed_rows):
    batch_rows, part, nvir = back.shape
    nao = virt.shape[0]
    product = dot(back[...].reshape(batch_rows * part, nvir), virt[...], ((1,), (1,)))
    for w in range(nao // 128):
        cols = slice(w * 128, (w + 1) * 128)
        for i in range(batch_rows):
            mixed_rows[w, pl.ds(i, part, stride=batch_rows), :] = product[i * part : (i + 1) * part, cols]
        out[:, cols] = mixed_rows[w]


def on_device(half_factors, block_mask, virt_coef, occ_energy, virt_energy, pair_list, pair_count):
    slab, rounds, nao = half_factors.shape
    nvir = virt_coef.shape[1]
    slots = 8
    length = rounds * slab
    dma = pltpu.SemaphoreType.DMA
    smem = pl.BlockSpec(memory_space=pltpu.SMEM)
    vmem = pl.BlockSpec(memory_space=pltpu.VMEM)
    anywhere = pl.BlockSpec(memory_space=pl.ANY)
    back = pl.pallas_call(
        pair_kernel,
        out_shape=jax.ShapeDtypeStruct((rounds, slab, nvir), jnp.bfloat16),
        in_specs=[smem, smem, smem, vmem, vmem, vmem, anywhere],
        out_specs=anywhere,
        scratch_shapes=[
            pltpu.VMEM((slab, rounds, nao), jnp.bfloat16),
            pltpu.VMEM((nvir // 128, length, 128), jnp.float32),
            pltpu.VMEM((rounds, slab, nvir), jnp.bfloat16),
            pltpu.VMEM((6, length, nvir), jnp.bfloat16),
            pltpu.VMEM((slots, nvir, nvir), jnp.float32),
            pltpu.VMEM((slots, nvir, nvir), jnp.float32),
            pltpu.VMEM((slots, nvir, nvir), jnp.bfloat16),
            pltpu.VMEM((length, nvir), jnp.bfloat16),
            pltpu.VMEM((length, nvir), jnp.bfloat16),
            pltpu.VMEM((length, nvir), jnp.bfloat16),
            pltpu.VMEM((nvir, 128), jnp.float32),
            pltpu.SMEM((slots,), jnp.float32),
            pltpu.SMEM((slots,), jnp.float32),
            dma((LOADS,)),
        ]
        + [dma((rounds,))] * 6
        + [dma((3, rounds))] * 2
        + [dma((rounds,))] * 4,
        compiler_params=pltpu.CompilerParams(
            collective_id=0, has_side_effects=True, vmem_limit_bytes=58 * 1024 * 1024
        ),
    )(occ_energy, pair_list, pair_count, block_mask, virt_energy[None, :], virt_coef, half_factors)

    steps = 4
    part = slab // steps
    wide_rows = pl.pallas_call(
        last_kernel,
        out_shape=jax.ShapeDtypeStruct((slab * rounds, nao), jnp.float32),
        grid=(steps,),
        in_specs=[
            pl.BlockSpec((rounds, part, nvir), lambda n: (0, n, 0)),
            pl.BlockSpec((nao, nvir), lambda n: (0, 0)),
        ],
        out_specs=pl.BlockSpec((part * rounds, nao), lambda n: (n, 0)),
        scratch_shapes=[pltpu.VMEM((nao // 128, part * rounds, 128), jnp.float32)],
        compiler_params=pltpu.CompilerParams(vmem_limit_bytes=32 * 1024 * 1024),
    )(back, virt_coef)
    return wide_rows.reshape(slab, rounds, nao)


def solution(mesh):
    in_specs = (P("aux", "obat", None), P("obat", None), P(), P(), P(), P(), P())
    out_specs = P("aux", "obat", None)
    return jax.shard_map(
        on_device, mesh=mesh, in_specs=in_specs, out_specs=out_specs, check_vma=False
    )
```

```python
import jax
import jax.numpy as jnp
from jax import lax
from jax.experimental import pallas as pl
from jax.experimental.pallas import tpu as pltpu
from jax.sharding import PartitionSpec as P

AOBLK = 64
SIDE = 4
AHEAD = 3
LAG_NEAR, LAG_FAR = 2, 3
LAG_SHARE = 2
LOADS = 4
ROWS = 16
SHIFTS = (
    (0, 0), (0, 1), (1, 0), (0, 3), (3, 0), (1, 1), (3, 3), (1, 3),
    (3, 1), (0, 2), (2, 0), (1, 2), (2, 1), (3, 2), (2, 3), (2, 2),
)
MESH = pl.DeviceIdType.MESH


def dot(a, b, contract=((1,), (0,))):
    return lax.dot_general(a, b, (contract, ((), ())), preferred_element_type=jnp.float32)


def look_up(axis, r):
    if isinstance(r, int):
        return SHIFTS[r][axis]
    found = jnp.int32(0)
    for k, steps in enumerate(SHIFTS):
        if steps[axis]:
            found += jnp.where(r == k, steps[axis], 0)
    return found


def pair_kernel(
    occ, listed, counted, mask, virt_row, virt, half, out, turned_out,
    half_vm, wide_f, local, panels, total, recip, mixed, share, opposite, gamma, virt_col, turned, sums, weight,
    l_sem, t_sem, a_send, a_recv, m_send, m_recv, p_send, p_recv, s_send, s_recv, g_send, g_recv, r_send, r_recv,
):
    aux = lax.axis_index("aux")
    obat = lax.axis_index("obat")
    y, x = aux // SIDE, aux % SIDE
    z, core = obat // 2, obat % 2
    rounds, slab, nvir = local.shape
    slots = total.shape[0]
    lanes = nvir // 128
    chunks = rounds // 2
    wide = 2 * slab
    z_one = (z + SIDE - 1 + 2 * core) % SIDE
    z_two = (z + 1 + 2 * core) % SIDE
    one = (aux, z_one * 2 + core)
    two = (aux, z_two * 2 + core)
    sibling = (aux, z * 2 + 1 - core)

    def shift(r):
        return look_up(0, r), look_up(1, r)

    def target(r):
        dy, dx = shift(r)
        return (y + dy) % SIDE * SIDE + (x + dx) % SIDE

    def source(r):
        dy, dx = shift(r)
        return (y + SIDE - dy) % SIDE * SIDE + (x + SIDE - dx) % SIDE

    def rows(r):
        return pl.ds(pl.multiple_of(r * slab, slab), slab)

    def chunk_rows(c):
        return pl.ds(pl.multiple_of(c * wide, wide), wide)

    def push(src, dst, send, recv, device):
        return pltpu.make_async_remote_copy(
            src_ref=src, dst_ref=dst, send_sem=send, recv_sem=recv,
            device_id=device, device_id_type=MESH,
        )

    def scatter(r):
        return push(local.at[r], panels.at[0, rows(r)], a_send.at[r], a_recv.at[r], (target(r), obat))

    def to_one(r):
        return push(panels.at[0, rows(r)], panels.at[4, rows(r)], m_send.at[r], m_recv.at[r], one)

    def to_two(r):
        return push(panels.at[0, rows(r)], panels.at[2, rows(r)], p_send.at[r], p_recv.at[r], two)

    def across(k, r):
        return push(
            panels.at[2 * k, rows(r)], panels.at[(1, 5, 3)[k], rows(r)],
            s_send.at[k, r], s_recv.at[k, r], sibling,
        )

    def give(r):
        return push(share.at[rows(r)], opposite.at[rows(r)], g_send.at[r], g_recv.at[r], one)

    def back(r):
        return push(gamma.at[rows(r)], out.at[aux], r_send.at[r], r_recv.at[r], (source(r), obat))

    piece = slab // LOADS

    def load(n):
        part = pl.ds(n * piece, piece)
        return pltpu.make_async_copy(half.at[part], half_vm.at[part], l_sem.at[n])

    for n in range(LOADS):
        load(n).start()

    barrier = pltpu.get_barrier_semaphore()

    def greet(r, carry):
        pl.semaphore_signal(barrier, inc=1, device_id=(target(r), obat), device_id_type=MESH)
        return carry

    lax.fori_loop(1, rounds, greet, 0)
    for device in (one, two, sibling):
        pl.semaphore_signal(barrier, inc=1, device_id=device, device_id_type=MESH)

    blocks = mask.shape[1]
    nao = virt.shape[0]
    spread = lax.broadcasted_iota(jnp.int32, (blocks, nao), 1) // AOBLK
    spread = (spread == lax.broadcasted_iota(jnp.int32, (blocks, nao), 0)).astype(jnp.bfloat16)
    keep = dot(mask[...].astype(jnp.bfloat16), spread).astype(jnp.bfloat16)
    for n in range(LOADS):
        load(n).wait()
        block = half_vm[pl.ds(n * piece, piece)] * keep[None]
        block = block.reshape(piece * rounds, nao)
        product = dot(block, virt[...])
        for w in range(lanes):
            wide_f[w, pl.ds(n * piece * rounds, piece * rounds), :] = product[:, w * 128 : (w + 1) * 128]

    def pick(r):
        parts = [wide_f[w, pl.ds(target(r), slab, stride=rounds), :] for w in range(lanes)]
        return jnp.concatenate(parts, axis=1).astype(jnp.bfloat16)

    panels[0, pl.ds(0, slab), :] = pick(0)
    pl.semaphore_wait(barrier, rounds + 2)

    def send_out(r, carry):
        local[r] = pick(r)
        scatter(r).start()
        return carry

    lax.fori_loop(1, 2 * AHEAD, send_out, 0)

    def orbital(level, side):
        return (level * 2 + side) * rounds + aux

    mine, foreign = orbital(z, core), orbital(z_one, core)
    couples = [(mine, orbital(level, side)) for level in (z, z_one, z_two) for side in (core, 1 - core)]
    couples += [(foreign, orbital(z_two, side)) for side in (core, 1 - core)]

    def prepare_scalars():
        for s, (i, j) in enumerate(couples):
            sums[s] = occ[i] + occ[j]
            hit = jnp.int32(0)
            for p in range(listed.shape[0]):
                hit += jnp.where((listed[p, i] == j) & (p < counted[i]), 1, 0)
            weight[s] = hit.astype(jnp.float32)

    def prepare(s, carry):
        total[s] = jnp.zeros((nvir, nvir), jnp.float32)
        for n in range(nvir // 128):
            cols = pl.ds(n * 128, 128)
            denom = (sums[s] - virt_col[...]) - virt_row[:, cols]
            recip[s, :, cols] = weight[s] / denom
        return carry

    def pair_up(c, held, fixed, others):
        part = chunk_rows(c)
        own = panels[fixed, part, :]
        flipped = (-own).T
        for t, s in zip(held, others):
            other = panels[s, part, :]
            total[t] += dot((2 * other).T, own) + dot(flipped, other)

    turned_copy = pltpu.make_async_copy(turned, turned_out, t_sem)

    def stage(c, carry):
        @pl.when(c < chunks)
        def _():
            for h in range(2):
                r = 2 * c + h
                if h == 0:
                    @pl.when(r > 0)
                    def _():
                        scatter(r).wait_recv()
                else:
                    scatter(r).wait_recv()
                to_one(r).start()
                to_two(r).start()
                across(0, r).start()

        @pl.when(c + AHEAD < chunks)
        def _():
            for h in range(2):
                send_out(2 * (c + AHEAD) + h, 0)

        @pl.when((c >= LAG_NEAR) & (c < chunks + LAG_NEAR))
        def _():
            for h in range(2):
                r = 2 * (c - LAG_NEAR) + h
                to_two(r).wait_recv()
                across(1, r).start()
                to_one(r).wait_recv()
                across(2, r).start()

        @pl.when(c == 0)
        def _():
            virt_col[...] = jnp.broadcast_to(virt_row[...], (128, nvir)).T
            turned[...] = virt[...].T
            turned_copy.start()
            prepare_scalars()
            lax.fori_loop(0, slots, prepare, 0)

        @pl.when((c >= LAG_NEAR) & (c < chunks + LAG_NEAR))
        def _():
            b = c - LAG_NEAR
            for h in range(2):
                across(0, 2 * b + h).wait_recv()
            pair_up(b, (0, 1, 2, 4), 0, (0, 1, 2, 4))
            pair_up(b, (6,), 2, (4,))

        @pl.when(c >= LAG_FAR)
        def _():
            b = c - LAG_FAR
            for h in range(2):
                across(1, 2 * b + h).wait_recv()
                across(2, 2 * b + h).wait_recv()
            pair_up(b, (3, 5), 0, (3, 5))
            pair_up(b, (7,), 2, (5,))

        return carry

    lax.fori_loop(0, chunks + LAG_FAR, stage, 0)

    def finish(s, carry):
        mixed[s] = (total[s] * recip[s]).astype(jnp.bfloat16)
        return carry

    halves = [pl.ds(n * (nvir // 2), nvir // 2) for n in range(2)]

    def collect(q, carry):
        @pl.when(q < chunks)
        def _():
            c = chunks - 1 - q
            part = chunk_rows(c)
            for cols in halves:
                acc = dot(panels[4, part, :], mixed[6, :, cols]) + dot(panels[5, part, :], mixed[7, :, cols])
                share[part, cols] = acc.astype(jnp.bfloat16)
            give(2 * c + 1).start()
            give(2 * c).start()

        @pl.when(q == 0)
        def _():
            lax.fori_loop(0, 6, finish, 0)

        @pl.when(q >= LAG_SHARE)
        def _():
            c = chunks - 1 - (q - LAG_SHARE)
            part = chunk_rows(c)
            give(2 * c + 1).wait_recv()
            give(2 * c).wait_recv()
            for cols in halves:
                acc = opposite[part, cols].astype(jnp.float32)
                for s in range(6):
                    acc += dot(panels[s, part, :], mixed[s, :, cols])
                gamma[part, cols] = acc.astype(jnp.bfloat16)
            back(2 * c + 1).start()

            @pl.when(c > 0)
            def _():
                back(2 * c).start()

        return carry

    lax.fori_loop(6, slots, finish, 0)
    lax.fori_loop(0, chunks + LAG_SHARE, collect, 0)
    own_copy = pltpu.make_async_copy(gamma.at[pl.ds(0, slab)], out.at[aux], r_send.at[0])
    own_copy.start()

    def settle(r, carry):
        to_one(r).wait_send()
        to_two(r).wait_send()
        give(r).wait_send()
        for k in range(3):
            across(k, r).wait_send()
        return carry

    lax.fori_loop(0, rounds, settle, 0)

    def close(r, carry):
        scatter(r).wait_send()
        back(r).wait()
        return carry

    own_copy.wait()
    turned_copy.wait()
    lax.fori_loop(1, rounds, close, 0)


def last_kernel(back, turned, out, back_vm, turned_vm, rows_vm, b_sem, t_sem, o_sem):
    batch_rows, slab, nvir = back.shape
    size = batch_rows * ROWS
    parts = slab // ROWS

    def bring(n):
        part = pl.ds(n * ROWS, ROWS)
        return pltpu.make_async_copy(back.at[:, part], back_vm.at[:, part], b_sem.at[n])

    def store(n):
        part = pl.ds(n * size, size)
        return pltpu.make_async_copy(rows_vm.at[part], out.at[part], o_sem.at[n])

    turned_copy = pltpu.make_async_copy(turned, turned_vm, t_sem)
    bring(0).start()
    turned_copy.start()
    for n in range(1, parts):
        bring(n).start()
    to_row = lax.broadcasted_iota(jnp.int32, (size, size), 0)
    from_row = lax.broadcasted_iota(jnp.int32, (size, size), 1)
    order = from_row == to_row % batch_rows * ROWS + to_row // batch_rows
    order = order.astype(jnp.float32).astype(jnp.bfloat16)
    turned_copy.wait()
    for n in range(parts):
        bring(n).wait()
        block = back_vm[:, n * ROWS : (n + 1) * ROWS, :].reshape(size, nvir)
        block = dot(order, block).astype(jnp.bfloat16)
        rows_vm[n * size : (n + 1) * size, :] = dot(block, turned_vm[...])
        store(n).start()
    for n in range(parts):
        store(n).wait()


def on_device(half_factors, block_mask, virt_coef, occ_energy, virt_energy, pair_list, pair_count):
    slab, rounds, nao = half_factors.shape
    nvir = virt_coef.shape[1]
    slots = 8
    length = rounds * slab
    dma = pltpu.SemaphoreType.DMA
    smem = pl.BlockSpec(memory_space=pltpu.SMEM)
    vmem = pl.BlockSpec(memory_space=pltpu.VMEM)
    anywhere = pl.BlockSpec(memory_space=pl.ANY)
    back, turned = pl.pallas_call(
        pair_kernel,
        out_shape=(
            jax.ShapeDtypeStruct((rounds, slab, nvir), jnp.bfloat16),
            jax.ShapeDtypeStruct((nvir, nao), jnp.bfloat16),
        ),
        in_specs=[smem, smem, smem, vmem, vmem, vmem, anywhere],
        out_specs=(anywhere, anywhere),
        scratch_shapes=[
            pltpu.VMEM((slab, rounds, nao), jnp.bfloat16),
            pltpu.VMEM((nvir // 128, length, 128), jnp.float32),
            pltpu.VMEM((rounds, slab, nvir), jnp.bfloat16),
            pltpu.VMEM((6, length, nvir), jnp.bfloat16),
            pltpu.VMEM((slots, nvir, nvir), jnp.float32),
            pltpu.VMEM((slots, nvir, nvir), jnp.float32),
            pltpu.VMEM((slots, nvir, nvir), jnp.bfloat16),
            pltpu.VMEM((length, nvir), jnp.bfloat16),
            pltpu.VMEM((length, nvir), jnp.bfloat16),
            pltpu.VMEM((length, nvir), jnp.bfloat16),
            pltpu.VMEM((nvir, 128), jnp.float32),
            pltpu.VMEM((nvir, nao), jnp.bfloat16),
            pltpu.SMEM((slots,), jnp.float32),
            pltpu.SMEM((slots,), jnp.float32),
            dma((LOADS,)),
            dma,
        ]
        + [dma((rounds,))] * 6
        + [dma((3, rounds))] * 2
        + [dma((rounds,))] * 4,
        compiler_params=pltpu.CompilerParams(
            collective_id=0, has_side_effects=True, vmem_limit_bytes=58 * 1024 * 1024
        ),
    )(occ_energy, pair_list.T, pair_count, block_mask, virt_energy[None, :], virt_coef, half_factors)

    parts = slab // ROWS
    wide_rows = pl.pallas_call(
        last_kernel,
        out_shape=jax.ShapeDtypeStruct((length, nao), jnp.float32),
        in_specs=[anywhere, anywhere],
        out_specs=anywhere,
        scratch_shapes=[
            pltpu.VMEM((rounds, slab, nvir), jnp.bfloat16),
            pltpu.VMEM((nvir, nao), jnp.bfloat16),
            pltpu.VMEM((length, nao), jnp.float32),
            dma((parts,)),
            dma,
            dma((parts,)),
        ],
        compiler_params=pltpu.CompilerParams(vmem_limit_bytes=60 * 1024 * 1024),
    )(back, turned)
    return wide_rows.reshape(slab, rounds, nao)


def solution(mesh):
    in_specs = (P("aux", "obat", None), P("obat", None), P(), P(), P(), P(), P())
    out_specs = P("aux", "obat", None)
    return jax.shard_map(
        on_device, mesh=mesh, in_specs=in_specs, out_specs=out_specs, check_vma=False
    )
```

```python
import jax
import jax.numpy as jnp
from jax import lax
from jax.experimental import pallas as pl
from jax.experimental.pallas import tpu as pltpu
from jax.sharding import PartitionSpec as P

AOBLK = 64
SIDE = 4
AHEAD = 3
LAG_NEAR, LAG_FAR = 2, 3
SPAN = 1
LAG_SHARE = 3
LOADS = 4
ROWS = 16
SHIFTS = (
    (0, 0), (0, 1), (1, 0), (0, 3), (3, 0), (1, 1), (3, 3), (1, 3),
    (3, 1), (0, 2), (2, 0), (1, 2), (2, 1), (3, 2), (2, 3), (2, 2),
)
MESH = pl.DeviceIdType.MESH


def dot(a, b, contract=((1,), (0,))):
    return lax.dot_general(a, b, (contract, ((), ())), preferred_element_type=jnp.float32)


def look_up(axis, r):
    if isinstance(r, int):
        return SHIFTS[r][axis]
    found = jnp.int32(0)
    for k, steps in enumerate(SHIFTS):
        if steps[axis]:
            found += jnp.where(r == k, steps[axis], 0)
    return found


def pair_kernel(
    occ, listed, counted, mask, virt_row, virt, half, out,
    half_vm, wide_f, local, panels, total, recip, mixed, share, opposite, gamma, virt_col, order, arrived, lined_up, sums, weight,
    l_sem, o_sem, a_send, a_recv, m_send, m_recv, p_send, p_recv, s_send, s_recv, g_send, g_recv, r_send, r_recv,
):
    aux = lax.axis_index("aux")
    obat = lax.axis_index("obat")
    y, x = aux // SIDE, aux % SIDE
    z, core = obat // 2, obat % 2
    rounds, slab, nvir = local.shape
    slots = total.shape[0]
    lanes = nvir // 128
    chunks = rounds // 2
    wide = 2 * slab
    z_one = (z + SIDE - 1 + 2 * core) % SIDE
    z_two = (z + 1 + 2 * core) % SIDE
    one = (aux, z_one * 2 + core)
    two = (aux, z_two * 2 + core)
    sibling = (aux, z * 2 + 1 - core)

    def shift(r):
        return look_up(0, r), look_up(1, r)

    def target(r):
        dy, dx = shift(r)
        return (y + dy) % SIDE * SIDE + (x + dx) % SIDE

    def source(r):
        dy, dx = shift(r)
        return (y + SIDE - dy) % SIDE * SIDE + (x + SIDE - dx) % SIDE

    def rows(r):
        return pl.ds(pl.multiple_of(r * slab, slab), slab)

    def chunk_rows(c):
        return pl.ds(pl.multiple_of(c * wide, wide), wide)

    def push(src, dst, send, recv, device):
        return pltpu.make_async_remote_copy(
            src_ref=src, dst_ref=dst, send_sem=send, recv_sem=recv,
            device_id=device, device_id_type=MESH,
        )

    def scatter(r):
        return push(local.at[r], panels.at[0, rows(r)], a_send.at[r], a_recv.at[r], (target(r), obat))

    def to_one(r):
        return push(panels.at[0, rows(r)], panels.at[4, rows(r)], m_send.at[r], m_recv.at[r], one)

    def to_two(r):
        return push(panels.at[0, rows(r)], panels.at[2, rows(r)], p_send.at[r], p_recv.at[r], two)

    def across(k, r):
        return push(
            panels.at[2 * k, rows(r)], panels.at[(1, 5, 3)[k], rows(r)],
            s_send.at[k, r], s_recv.at[k, r], sibling,
        )

    def give(r):
        return push(share.at[rows(r)], opposite.at[rows(r)], g_send.at[r], g_recv.at[r], one)

    def back(r):
        return push(gamma.at[rows(r)], arrived.at[aux], r_send.at[r], r_recv.at[r], (source(r), obat))

    piece = slab // LOADS

    def load(n):
        part = pl.ds(n * piece, piece)
        return pltpu.make_async_copy(half.at[part], half_vm.at[part], l_sem.at[n])

    for n in range(LOADS):
        load(n).start()

    barrier = pltpu.get_barrier_semaphore()

    def greet(r, carry):
        pl.semaphore_signal(barrier, inc=1, device_id=(target(r), obat), device_id_type=MESH)
        return carry

    lax.fori_loop(1, rounds, greet, 0)
    for device in (one, two, sibling):
        pl.semaphore_signal(barrier, inc=1, device_id=device, device_id_type=MESH)

    blocks = mask.shape[1]
    nao = virt.shape[0]
    spread = lax.broadcasted_iota(jnp.int32, (blocks, nao), 1) // AOBLK
    spread = (spread == lax.broadcasted_iota(jnp.int32, (blocks, nao), 0)).astype(jnp.bfloat16)
    keep = dot(mask[...].astype(jnp.bfloat16), spread).astype(jnp.bfloat16)
    for n in range(LOADS):
        load(n).wait()
        block = half_vm[pl.ds(n * piece, piece)] * keep[None]
        block = block.reshape(piece * rounds, nao)
        product = dot(block, virt[...])
        for w in range(lanes):
            wide_f[w, pl.ds(n * piece * rounds, piece * rounds), :] = product[:, w * 128 : (w + 1) * 128]

    def pick(r):
        parts = [wide_f[w, pl.ds(target(r), slab, stride=rounds), :] for w in range(lanes)]
        return jnp.concatenate(parts, axis=1).astype(jnp.bfloat16)

    panels[0, pl.ds(0, slab), :] = pick(0)
    pl.semaphore_wait(barrier, rounds + 2)

    def send_out(r, carry):
        local[r] = pick(r)
        scatter(r).start()
        return carry

    lax.fori_loop(1, 2 * AHEAD, send_out, 0)

    def orbital(level, side):
        return (level * 2 + side) * rounds + aux

    mine, foreign = orbital(z, core), orbital(z_one, core)
    couples = [(mine, orbital(level, side)) for level in (z, z_one, z_two) for side in (core, 1 - core)]
    couples += [(foreign, orbital(z_two, side)) for side in (core, 1 - core)]

    def prepare_scalars():
        for s, (i, j) in enumerate(couples):
            sums[s] = occ[i] + occ[j]
            hit = jnp.int32(0)
            for p in range(listed.shape[0]):
                hit += jnp.where((listed[p, i] == j) & (p < counted[i]), 1, 0)
            weight[s] = hit.astype(jnp.float32)

    def prepare(s, carry):
        total[s] = jnp.zeros((nvir, nvir), jnp.float32)
        for n in range(nvir // 128):
            cols = pl.ds(n * 128, 128)
            denom = (sums[s] - virt_col[...]) - virt_row[:, cols]
            recip[s, :, cols] = weight[s] / denom
        return carry

    def pair_up(c, held, fixed, others):
        part = chunk_rows(c)
        own = panels[fixed, part, :]
        flipped = (-own).T
        for t, s in zip(held, others):
            other = panels[s, part, :]
            total[t] += dot((2 * other).T, own) + dot(flipped, other)

    size = rounds * ROWS

    def plan_order():
        to_row = lax.broadcasted_iota(jnp.int32, (size, size), 0)
        from_row = lax.broadcasted_iota(jnp.int32, (size, size), 1)
        hit = from_row == to_row % rounds * ROWS + to_row // rounds
        order[...] = hit.astype(jnp.float32).astype(jnp.bfloat16)

    def stage(c, carry):
        @pl.when(c < chunks)
        def _():
            for h in range(2):
                r = 2 * c + h
                if h == 0:
                    @pl.when(r > 0)
                    def _():
                        scatter(r).wait_recv()
                else:
                    scatter(r).wait_recv()
                to_one(r).start()
                to_two(r).start()
                across(0, r).start()

        @pl.when(c + AHEAD < chunks)
        def _():
            for h in range(2):
                send_out(2 * (c + AHEAD) + h, 0)

        @pl.when((c >= LAG_NEAR) & (c < chunks + LAG_NEAR))
        def _():
            for h in range(2):
                r = 2 * (c - LAG_NEAR) + h
                to_two(r).wait_recv()
                across(1, r).start()
                to_one(r).wait_recv()
                across(2, r).start()

        @pl.when(c == 0)
        def _():
            virt_col[...] = jnp.broadcast_to(virt_row[...], (128, nvir)).T
            plan_order()
            prepare_scalars()
            lax.fori_loop(0, slots, prepare, 0)

        @pl.when((c >= LAG_NEAR) & (c < chunks + LAG_NEAR))
        def _():
            b = c - LAG_NEAR
            for h in range(2):
                across(0, 2 * b + h).wait_recv()
            pair_up(b, (0, 1, 2, 4), 0, (0, 1, 2, 4))
            pair_up(b, (6,), 2, (4,))

        @pl.when(c >= LAG_FAR)
        def _():
            b = c - LAG_FAR
            for h in range(2):
                across(1, 2 * b + h).wait_recv()
                across(2, 2 * b + h).wait_recv()
            pair_up(b, (3, 5), 0, (3, 5))
            pair_up(b, (7,), 2, (5,))

        return carry

    lax.fori_loop(0, chunks + LAG_FAR, stage, 0)

    def finish(s, carry):
        mixed[s] = (total[s] * recip[s]).astype(jnp.bfloat16)
        return carry

    halves = [pl.ds(n * (nvir // 2), nvir // 2) for n in range(2)]

    steps = rounds // SPAN

    def span_rows(c):
        return pl.ds(pl.multiple_of(c * SPAN * slab, SPAN * slab), SPAN * slab)

    def collect(q, carry):
        @pl.when(q < steps)
        def _():
            c = steps - 1 - q
            part = span_rows(c)
            for cols in halves:
                acc = dot(panels[4, part, :], mixed[6, :, cols]) + dot(panels[5, part, :], mixed[7, :, cols])
                share[part, cols] = acc.astype(jnp.bfloat16)
            for h in range(SPAN):
                give(SPAN * c + SPAN - 1 - h).start()

        @pl.when(q == 0)
        def _():
            lax.fori_loop(0, 6, finish, 0)

        @pl.when(q >= LAG_SHARE)
        def _():
            c = steps - 1 - (q - LAG_SHARE)
            part = span_rows(c)
            for h in range(SPAN):
                give(SPAN * c + SPAN - 1 - h).wait_recv()
            for cols in halves:
                acc = opposite[part, cols].astype(jnp.float32)
                for s in range(6):
                    acc += dot(panels[s, part, :], mixed[s, :, cols])
                gamma[part, cols] = acc.astype(jnp.bfloat16)
            for h in range(SPAN):
                r = SPAN * c + SPAN - 1 - h

                @pl.when(r > 0)
                def _():
                    back(r).start()

        return carry

    lax.fori_loop(6, slots, finish, 0)
    lax.fori_loop(0, steps + LAG_SHARE, collect, 0)
    arrived[aux] = gamma[pl.ds(0, slab), :]

    def land(r, carry):
        back(rounds - r).wait_recv()
        return carry

    lax.fori_loop(1, rounds, land, 0)

    def leave(n):
        part = pl.ds(n * size, size)
        return pltpu.make_async_copy(lined_up.at[part], out.at[part], o_sem.at[n])

    for n in range(slab // ROWS):
        block = arrived[:, n * ROWS : (n + 1) * ROWS, :].reshape(size, nvir)
        lined_up[pl.ds(n * size, size), :] = dot(order[...], block).astype(jnp.bfloat16)
        leave(n).start()

    def settle(r, carry):
        to_one(r).wait_send()
        to_two(r).wait_send()
        give(r).wait_send()
        for k in range(3):
            across(k, r).wait_send()
        return carry

    lax.fori_loop(0, rounds, settle, 0)

    def close(r, carry):
        scatter(r).wait_send()
        back(r).wait_send()
        return carry

    lax.fori_loop(1, rounds, close, 0)
    for n in range(slab // ROWS):
        leave(n).wait()


def on_device(half_factors, block_mask, virt_coef, occ_energy, virt_energy, pair_list, pair_count):
    slab, rounds, nao = half_factors.shape
    nvir = virt_coef.shape[1]
    slots = 8
    length = rounds * slab
    dma = pltpu.SemaphoreType.DMA
    smem = pl.BlockSpec(memory_space=pltpu.SMEM)
    vmem = pl.BlockSpec(memory_space=pltpu.VMEM)
    anywhere = pl.BlockSpec(memory_space=pl.ANY)
    back = pl.pallas_call(
        pair_kernel,
        out_shape=jax.ShapeDtypeStruct((length, nvir), jnp.bfloat16),
        in_specs=[smem, smem, smem, vmem, vmem, vmem, anywhere],
        out_specs=anywhere,
        scratch_shapes=[
            pltpu.VMEM((slab, rounds, nao), jnp.bfloat16),
            pltpu.VMEM((nvir // 128, length, 128), jnp.float32),
            pltpu.VMEM((rounds, slab, nvir), jnp.bfloat16),
            pltpu.VMEM((6, length, nvir), jnp.bfloat16),
            pltpu.VMEM((slots, nvir, nvir), jnp.float32),
            pltpu.VMEM((slots, nvir, nvir), jnp.float32),
            pltpu.VMEM((slots, nvir, nvir), jnp.bfloat16),
            pltpu.VMEM((length, nvir), jnp.bfloat16),
            pltpu.VMEM((length, nvir), jnp.bfloat16),
            pltpu.VMEM((length, nvir), jnp.bfloat16),
            pltpu.VMEM((nvir, 128), jnp.float32),
            pltpu.VMEM((rounds * ROWS, rounds * ROWS), jnp.bfloat16),
            pltpu.VMEM((rounds, slab, nvir), jnp.bfloat16),
            pltpu.VMEM((length, nvir), jnp.bfloat16),
            pltpu.SMEM((slots,), jnp.float32),
            pltpu.SMEM((slots,), jnp.float32),
            dma((LOADS,)),
            dma((slab // ROWS,)),
        ]
        + [dma((rounds,))] * 6
        + [dma((3, rounds))] * 2
        + [dma((rounds,))] * 4,
        compiler_params=pltpu.CompilerParams(
            collective_id=0, has_side_effects=True, vmem_limit_bytes=58 * 1024 * 1024
        ),
    )(occ_energy, pair_list.T, pair_count, block_mask, virt_energy[None, :], virt_coef, half_factors)

    wide_rows = dot(back, virt_coef, ((1,), (1,)))
    return wide_rows.reshape(slab, rounds, nao)


def solution(mesh):
    in_specs = (P("aux", "obat", None), P("obat", None), P(), P(), P(), P(), P())
    out_specs = P("aux", "obat", None)
    return jax.shard_map(
        on_device, mesh=mesh, in_specs=in_specs, out_specs=out_specs, check_vma=False
    )
```

```python
import jax
import jax.numpy as jnp
from jax import lax
from jax.experimental import pallas as pl
from jax.experimental.pallas import tpu as pltpu
from jax.sharding import PartitionSpec as P

AOBLK = 64
SIDE = 4
AHEAD = 3
LAG_OWN, LAG_NEAR, LAG_FAR = 1, 2, 3
SPAN = 1
LAG_SHARE = 3
LOADS = 4
ROWS = 16
SHIFTS = (
    (0, 0), (0, 1), (1, 0), (0, 3), (3, 0), (1, 1), (3, 3), (1, 3),
    (3, 1), (0, 2), (2, 0), (1, 2), (2, 1), (3, 2), (2, 3), (2, 2),
)
MESH = pl.DeviceIdType.MESH


def dot(a, b, contract=((1,), (0,))):
    return lax.dot_general(a, b, (contract, ((), ())), preferred_element_type=jnp.float32)


def look_up(axis, r):
    if isinstance(r, int):
        return SHIFTS[r][axis]
    found = jnp.int32(0)
    for k, steps in enumerate(SHIFTS):
        if steps[axis]:
            found += jnp.where(r == k, steps[axis], 0)
    return found


def pair_kernel(
    occ, listed, counted, mask, virt_row, virt, half, out,
    half_vm, wide_f, local, panels, total, recip, mixed, share, opposite, gamma, virt_col, order, arrived, lined_up, sums, weight,
    l_sem, o_sem, a_send, a_recv, m_send, m_recv, p_send, p_recv, s_send, s_recv, g_send, g_recv, r_send, r_recv,
):
    aux = lax.axis_index("aux")
    obat = lax.axis_index("obat")
    y, x = aux // SIDE, aux % SIDE
    z, core = obat // 2, obat % 2
    rounds, slab, nvir = local.shape
    slots = total.shape[0]
    lanes = nvir // 128
    chunks = rounds // 2
    wide = 2 * slab
    z_one = (z + SIDE - 1 + 2 * core) % SIDE
    z_two = (z + 1 + 2 * core) % SIDE
    one = (aux, z_one * 2 + core)
    two = (aux, z_two * 2 + core)
    sibling = (aux, z * 2 + 1 - core)

    def shift(r):
        return look_up(0, r), look_up(1, r)

    def target(r):
        dy, dx = shift(r)
        return (y + dy) % SIDE * SIDE + (x + dx) % SIDE

    def source(r):
        dy, dx = shift(r)
        return (y + SIDE - dy) % SIDE * SIDE + (x + SIDE - dx) % SIDE

    def rows(r):
        return pl.ds(pl.multiple_of(r * slab, slab), slab)

    def chunk_rows(c):
        return pl.ds(pl.multiple_of(c * wide, wide), wide)

    def push(src, dst, send, recv, device):
        return pltpu.make_async_remote_copy(
            src_ref=src, dst_ref=dst, send_sem=send, recv_sem=recv,
            device_id=device, device_id_type=MESH,
        )

    def scatter(r):
        return push(local.at[r], panels.at[0, rows(r)], a_send.at[r], a_recv.at[r], (target(r), obat))

    def to_one(r):
        return push(panels.at[0, rows(r)], panels.at[4, rows(r)], m_send.at[r], m_recv.at[r], one)

    def to_two(r):
        return push(panels.at[0, rows(r)], panels.at[2, rows(r)], p_send.at[r], p_recv.at[r], two)

    def across(k, r):
        return push(
            panels.at[2 * k, rows(r)], panels.at[(1, 5, 3)[k], rows(r)],
            s_send.at[k, r], s_recv.at[k, r], sibling,
        )

    def give(r):
        return push(share.at[rows(r)], opposite.at[rows(r)], g_send.at[r], g_recv.at[r], one)

    def back(r):
        return push(gamma.at[rows(r)], arrived.at[aux], r_send.at[r], r_recv.at[r], (source(r), obat))

    piece = slab // LOADS

    def load(n):
        part = pl.ds(n * piece, piece)
        return pltpu.make_async_copy(half.at[part], half_vm.at[part], l_sem.at[n])

    for n in range(LOADS):
        load(n).start()

    barrier = pltpu.get_barrier_semaphore()

    def greet(r, carry):
        pl.semaphore_signal(barrier, inc=1, device_id=(target(r), obat), device_id_type=MESH)
        return carry

    lax.fori_loop(1, rounds, greet, 0)
    for device in (one, two, sibling):
        pl.semaphore_signal(barrier, inc=1, device_id=device, device_id_type=MESH)

    blocks = mask.shape[1]
    nao = virt.shape[0]
    spread = lax.broadcasted_iota(jnp.int32, (blocks, nao), 1) // AOBLK
    spread = (spread == lax.broadcasted_iota(jnp.int32, (blocks, nao), 0)).astype(jnp.bfloat16)
    keep = dot(mask[...].astype(jnp.bfloat16), spread).astype(jnp.bfloat16)
    for n in range(LOADS):
        load(n).wait()
        block = half_vm[pl.ds(n * piece, piece)] * keep[None]
        block = block.reshape(piece * rounds, nao)
        product = dot(block, virt[...])
        for w in range(lanes):
            wide_f[w, pl.ds(n * piece * rounds, piece * rounds), :] = product[:, w * 128 : (w + 1) * 128]

    def pick(r):
        parts = [wide_f[w, pl.ds(target(r), slab, stride=rounds), :] for w in range(lanes)]
        return jnp.concatenate(parts, axis=1).astype(jnp.bfloat16)

    panels[0, pl.ds(0, slab), :] = pick(0)
    pl.semaphore_wait(barrier, rounds + 2)

    def send_out(r, carry):
        local[r] = pick(r)
        scatter(r).start()
        return carry

    lax.fori_loop(1, 2 * AHEAD, send_out, 0)

    def orbital(level, side):
        return (level * 2 + side) * rounds + aux

    mine, foreign = orbital(z, core), orbital(z_one, core)
    couples = [(mine, orbital(level, side)) for level in (z, z_one, z_two) for side in (core, 1 - core)]
    couples += [(foreign, orbital(z_two, side)) for side in (core, 1 - core)]

    def prepare_scalars():
        for s, (i, j) in enumerate(couples):
            sums[s] = occ[i] + occ[j]
            hit = jnp.int32(0)
            for p in range(listed.shape[0]):
                hit += jnp.where((listed[p, i] == j) & (p < counted[i]), 1, 0)
            weight[s] = hit.astype(jnp.float32)

    def prepare(s, carry):
        total[s] = jnp.zeros((nvir, nvir), jnp.float32)
        for n in range(nvir // 128):
            cols = pl.ds(n * 128, 128)
            denom = (sums[s] - virt_col[...]) - virt_row[:, cols]
            recip[s, :, cols] = weight[s] / denom
        return carry

    def pair_up(c, held, fixed, others):
        part = chunk_rows(c)
        own = panels[fixed, part, :]
        flipped = (-own).T
        for t, s in zip(held, others):
            other = panels[s, part, :]
            total[t] += dot((2 * other).T, own) + dot(flipped, other)

    size = rounds * ROWS

    def plan_order():
        to_row = lax.broadcasted_iota(jnp.int32, (size, size), 0)
        from_row = lax.broadcasted_iota(jnp.int32, (size, size), 1)
        hit = from_row == to_row % rounds * ROWS + to_row // rounds
        order[...] = hit.astype(jnp.float32).astype(jnp.bfloat16)

    def stage(c, carry):
        @pl.when(c < chunks)
        def _():
            for h in range(2):
                r = 2 * c + h
                if h == 0:
                    @pl.when(r > 0)
                    def _():
                        scatter(r).wait_recv()
                else:
                    scatter(r).wait_recv()
                to_one(r).start()
                to_two(r).start()
                across(0, r).start()

        @pl.when(c + AHEAD < chunks)
        def _():
            for h in range(2):
                send_out(2 * (c + AHEAD) + h, 0)

        @pl.when(c == 0)
        def _():
            virt_col[...] = jnp.broadcast_to(virt_row[...], (128, nvir)).T
            plan_order()
            prepare_scalars()
            lax.fori_loop(0, slots, prepare, 0)

        @pl.when((c >= LAG_OWN) & (c < chunks + LAG_OWN))
        def _():
            b = c - LAG_OWN
            for h in range(2):
                across(0, 2 * b + h).wait_recv()
            pair_up(b, (0, 1), 0, (0, 1))

        @pl.when(c >= LAG_FAR)
        def _():
            b = c - LAG_FAR
            for h in range(2):
                across(1, 2 * b + h).wait_recv()
                across(2, 2 * b + h).wait_recv()
            pair_up(b, (3, 5), 0, (3, 5))
            pair_up(b, (7,), 2, (5,))

        @pl.when((c >= LAG_NEAR) & (c < chunks + LAG_NEAR))
        def _():
            b = c - LAG_NEAR
            for h in range(2):
                r = 2 * b + h
                to_two(r).wait_recv()
                across(1, r).start()
                to_one(r).wait_recv()
                across(2, r).start()
            pair_up(b, (2, 4), 0, (2, 4))
            pair_up(b, (6,), 2, (4,))

        return carry

    lax.fori_loop(0, chunks + LAG_FAR, stage, 0)

    def finish(s, carry):
        mixed[s] = (total[s] * recip[s]).astype(jnp.bfloat16)
        return carry

    halves = [pl.ds(n * (nvir // 2), nvir // 2) for n in range(2)]

    steps = rounds // SPAN

    def span_rows(c):
        return pl.ds(pl.multiple_of(c * SPAN * slab, SPAN * slab), SPAN * slab)

    def collect(q, carry):
        @pl.when(q < steps)
        def _():
            c = steps - 1 - q
            part = span_rows(c)
            for cols in halves:
                acc = dot(panels[4, part, :], mixed[6, :, cols]) + dot(panels[5, part, :], mixed[7, :, cols])
                share[part, cols] = acc.astype(jnp.bfloat16)
            for h in range(SPAN):
                give(SPAN * c + SPAN - 1 - h).start()

        @pl.when(q == 0)
        def _():
            lax.fori_loop(0, 6, finish, 0)

        @pl.when(q >= LAG_SHARE)
        def _():
            c = steps - 1 - (q - LAG_SHARE)
            part = span_rows(c)
            for h in range(SPAN):
                give(SPAN * c + SPAN - 1 - h).wait_recv()
            for cols in halves:
                acc = opposite[part, cols].astype(jnp.float32)
                for s in range(6):
                    acc += dot(panels[s, part, :], mixed[s, :, cols])
                gamma[part, cols] = acc.astype(jnp.bfloat16)
            for h in range(SPAN):
                r = SPAN * c + SPAN - 1 - h

                @pl.when(r > 0)
                def _():
                    back(r).start()

        return carry

    lax.fori_loop(6, slots, finish, 0)
    lax.fori_loop(0, steps + LAG_SHARE, collect, 0)
    arrived[aux] = gamma[pl.ds(0, slab), :]

    def land(r, carry):
        back(rounds - r).wait_recv()
        return carry

    lax.fori_loop(1, rounds, land, 0)

    def leave(n):
        part = pl.ds(n * size, size)
        return pltpu.make_async_copy(lined_up.at[part], out.at[part], o_sem.at[n])

    for n in range(slab // ROWS):
        block = arrived[:, n * ROWS : (n + 1) * ROWS, :].reshape(size, nvir)
        lined_up[pl.ds(n * size, size), :] = dot(order[...], block).astype(jnp.bfloat16)
        leave(n).start()

    def settle(r, carry):
        to_one(r).wait_send()
        to_two(r).wait_send()
        give(r).wait_send()
        for k in range(3):
            across(k, r).wait_send()
        return carry

    lax.fori_loop(0, rounds, settle, 0)

    def close(r, carry):
        scatter(r).wait_send()
        back(r).wait_send()
        return carry

    lax.fori_loop(1, rounds, close, 0)
    for n in range(slab // ROWS):
        leave(n).wait()


def on_device(half_factors, block_mask, virt_coef, occ_energy, virt_energy, pair_list, pair_count):
    slab, rounds, nao = half_factors.shape
    nvir = virt_coef.shape[1]
    slots = 8
    length = rounds * slab
    dma = pltpu.SemaphoreType.DMA
    smem = pl.BlockSpec(memory_space=pltpu.SMEM)
    vmem = pl.BlockSpec(memory_space=pltpu.VMEM)
    anywhere = pl.BlockSpec(memory_space=pl.ANY)
    back = pl.pallas_call(
        pair_kernel,
        out_shape=jax.ShapeDtypeStruct((length, nvir), jnp.bfloat16),
        in_specs=[smem, smem, smem, vmem, vmem, vmem, anywhere],
        out_specs=anywhere,
        scratch_shapes=[
            pltpu.VMEM((slab, rounds, nao), jnp.bfloat16),
            pltpu.VMEM((nvir // 128, length, 128), jnp.float32),
            pltpu.VMEM((rounds, slab, nvir), jnp.bfloat16),
            pltpu.VMEM((6, length, nvir), jnp.bfloat16),
            pltpu.VMEM((slots, nvir, nvir), jnp.float32),
            pltpu.VMEM((slots, nvir, nvir), jnp.float32),
            pltpu.VMEM((slots, nvir, nvir), jnp.bfloat16),
            pltpu.VMEM((length, nvir), jnp.bfloat16),
            pltpu.VMEM((length, nvir), jnp.bfloat16),
            pltpu.VMEM((length, nvir), jnp.bfloat16),
            pltpu.VMEM((nvir, 128), jnp.float32),
            pltpu.VMEM((rounds * ROWS, rounds * ROWS), jnp.bfloat16),
            pltpu.VMEM((rounds, slab, nvir), jnp.bfloat16),
            pltpu.VMEM((length, nvir), jnp.bfloat16),
            pltpu.SMEM((slots,), jnp.float32),
            pltpu.SMEM((slots,), jnp.float32),
            dma((LOADS,)),
            dma((slab // ROWS,)),
        ]
        + [dma((rounds,))] * 6
        + [dma((3, rounds))] * 2
        + [dma((rounds,))] * 4,
        compiler_params=pltpu.CompilerParams(
            collective_id=0, has_side_effects=True, vmem_limit_bytes=58 * 1024 * 1024
        ),
    )(occ_energy, pair_list.T, pair_count, block_mask, virt_energy[None, :], virt_coef, half_factors)

    wide_rows = dot(back, virt_coef, ((1,), (1,)))
    return wide_rows.reshape(slab, rounds, nao)


def solution(mesh):
    in_specs = (P("aux", "obat", None), P("obat", None), P(), P(), P(), P(), P())
    out_specs = P("aux", "obat", None)
    return jax.shard_map(
        on_device, mesh=mesh, in_specs=in_specs, out_specs=out_specs, check_vma=False
    )
```
